32 devices in a mesh: seq: 8 (over y, x, core), clip: 4 (over z).
Axes of the slice: x: 2, y: 2, z: 4, core: 2. Of those that a mesh axis runs over, the one named last changes fastest.
Arguments:
- frames_in: bfloat16 [4, 8, 128, 768], P('clip', 'seq'), may hold values from -6 to 6
- norm_gains: float32 [2, 768], replicated, may hold values from 0.5 to 1.5
- space_proj: bfloat16 [768, 2304], replicated, may hold values from -0.21875 to 0.21875
- space_out: bfloat16 [768, 768], replicated, may hold values from -0.21875 to 0.21875
- time_proj: bfloat16 [768, 2304], replicated, may hold values from -0.21875 to 0.21875
- time_out: bfloat16 [768, 768], replicated, may hold values from -0.21875 to 0.21875
- qk_gains: float32 [4, 768], replicated, may hold values from 1 to 2.5
Outputs:
- block_out: bfloat16 [4, 8, 128, 768], P('clip', 'seq')
- clip_embed: float32 [4, 768], P('clip')
- similarity: float32 [4, 4], P('clip')
The draws below stay inside these ranges and needn't reach their ends.
All inputs are finite; a program needn't handle non-finite values.
Results may differ from the reference program's by a relative error of at most 0.02.
Values may be sent and summed in bfloat16 or wider, within the bound.
A program may use at most 64 MiB of HBM per device.

```python
import math
import jax
import jax.numpy as jnp
from jax import lax

D = 768
HEADS = 12
PATCHES = 128
FRAMES = 8
CLIPS = 4


def level_of(rng, shape, shards, least, high):
    def one(axis_at, blocks):
        heights = jax.random.uniform(jax.random.fold_in(jax.random.fold_in(rng, 6), axis_at), (blocks,), jnp.float32, least / len(shards), high / len(shards))
        return jnp.repeat(jnp.exp(heights), shape[axis_at] // blocks).reshape((-1,) + (1,) * (len(shape) - axis_at - 1))

    factor_of = one(*shards[0])
    for cut in shards[1:]:
        factor_of = factor_of * one(*cut)
    return factor_of


def bell_draw(rng, shape, scale, reach, shards=(), kind=jnp.bfloat16):
    values = scale * jax.random.normal(rng, shape, jnp.float32)
    if shards:
        values = values * level_of(rng, shape, shards, -0.22, 0.18)
    return jnp.clip(values, -reach, reach).astype(kind)


def setup_inputs(seed: int = 0) -> dict:
    arg_keys = jax.random.split(jax.random.key(seed), 8)
    return {
        "frames_in": bell_draw(arg_keys[0], (CLIPS, FRAMES, PATCHES, D), 1.0, 6.0, ((0, 4), (1, 8))),
        "norm_gains": jnp.clip(1.0 + 0.1 * jax.random.normal(arg_keys[1], (2, D), jnp.float32), 0.5, 1.5),
        "space_proj": bell_draw(arg_keys[2], (D, 3 * D), D ** -0.5, 0.21875),
        "space_out": bell_draw(arg_keys[3], (D, D), D ** -0.5, 0.21875),
        "time_proj": bell_draw(arg_keys[4], (D, 3 * D), D ** -0.5, 0.21875),
        "time_out": bell_draw(arg_keys[5], (D, D), D ** -0.5, 0.21875),
        "qk_gains": jnp.clip(jax.random.uniform(arg_keys[6], (4, D), jnp.float32, 1.0, 2.5), 1.0, 2.5),
    }


def layer_norm(values, gains_row):
    widened = values.astype(jnp.float32)
    average = lax.optimization_barrier(jnp.mean(widened, axis=-1, keepdims=True))
    centred = widened - average
    spread = lax.optimization_barrier(jnp.mean(centred * centred, axis=-1, keepdims=True))
    return (centred * lax.rsqrt(spread + 1e-05) * gains_row).astype(jnp.bfloat16)

def head_norm(values, gains_row):
    inverse = lax.rsqrt(lax.optimization_barrier(jnp.mean(values * values, axis=-1, keepdims=True)) + 1e-06)
    return (values * inverse * gains_row.reshape(HEADS, -1)).astype(jnp.bfloat16)

def attention(normed, proj, out_weight, gain_query, gain_key):
    channels = normed.shape[-1]
    leading = normed.shape[:-1]
    head_size = channels // HEADS
    projected = jnp.dot(normed.reshape(-1, channels), proj, preferred_element_type=jnp.float32)
    projected = projected.astype(jnp.bfloat16).reshape(leading + (3 * channels,))
    queries = projected[..., :channels].astype(jnp.float32).reshape(leading + (HEADS, head_size))
    key_part = projected[..., channels:2 * channels].astype(jnp.float32).reshape(leading + (HEADS, head_size))
    value_part = projected[..., 2 * channels:].reshape(leading + (HEADS, head_size))
    query_n = head_norm(queries, gain_query)
    key_n = head_norm(key_part, gain_key)
    scores = jnp.einsum('...lhe,...mhe->...hlm', query_n.astype(jnp.float32), key_n.astype(jnp.float32))
    scores = scores * (1.0 / math.sqrt(head_size))
    raised = jnp.exp(scores)
    attn_weights = (raised / lax.optimization_barrier(jnp.sum(raised, axis=-1, keepdims=True))).astype(jnp.bfloat16)
    context = jnp.einsum('...hlm,...mhe->...lhe', attn_weights.astype(jnp.float32), value_part.astype(jnp.float32))
    context = context.astype(jnp.bfloat16).reshape(-1, channels)
    branch = jnp.dot(context, out_weight, preferred_element_type=jnp.float32)
    return branch.reshape(leading + (channels,))

def reference(frames_in, norm_gains, space_proj, space_out, time_proj, time_out, qk_gains):

    def per_clip(clip_tokens):
        spatial_in = layer_norm(clip_tokens, norm_gains[0])
        branch = attention(spatial_in, space_proj, space_out, qk_gains[0], qk_gains[1])
        middle = (clip_tokens.astype(jnp.float32) + branch).astype(jnp.bfloat16)
        temporal_in = jnp.transpose(layer_norm(middle, norm_gains[1]), (1, 0, 2))
        temporal = attention(temporal_in, time_proj, time_out, qk_gains[2], qk_gains[3]).astype(jnp.bfloat16)
        temporal = jnp.transpose(temporal, (1, 0, 2))
        block_out = (middle.astype(jnp.float32) + temporal.astype(jnp.float32)).astype(jnp.bfloat16)
        pooled = lax.optimization_barrier(jnp.sum(block_out.astype(jnp.float32), axis=(0, 1))) / (FRAMES * PATCHES)
        return (block_out, pooled)
    block_out, pooled = lax.map(per_clip, frames_in)
    clip_embed = pooled * lax.rsqrt(lax.optimization_barrier(jnp.mean(pooled * pooled, axis=-1, keepdims=True)) + 1e-06)
    similarity = jnp.dot(clip_embed, clip_embed.T, precision=lax.Precision.HIGHEST, preferred_element_type=jnp.float32) / D
    return (block_out, clip_embed, similarity)
```

```python
import functools

import jax
import jax.numpy as jnp
from jax import lax
from jax.experimental import pallas as pl
from jax.experimental.pallas import tpu as pltpu
from jax.sharding import PartitionSpec as P

D = 768
HEADS = 12
HEAD = D // HEADS
WIDE = 4 * HEAD
MESH = pl.DeviceIdType.MESH
BF16 = jnp.bfloat16
F32 = jnp.float32


def each(count, body):
    if count <= 8:
        for at in range(1, count):
            body(at)
    else:
        lax.fori_loop(1, count, lambda at, carry: (body(at), carry)[1], 0)


def layer_norm(widened, gain):
    average = jnp.mean(widened, axis=-1, keepdims=True)
    centred = widened - average
    spread = jnp.mean(centred * centred, axis=-1, keepdims=True)
    return (centred * lax.rsqrt(spread + 1e-05) * gain).astype(BF16)


def attend(tokens, proj, out_weight, gains, query_row, mask, waits):
    row = lax.broadcasted_iota(jnp.int32, (WIDE, WIDE), 0) // HEAD
    col = lax.broadcasted_iota(jnp.int32, (WIDE, WIDE), 1) // HEAD
    averager = jnp.where(row == col, 1.0 / HEAD, 0.0).astype(BF16)
    count = tokens.shape[0]
    low = lax.broadcasted_iota(jnp.int32, (count, 2 * HEAD), 1) < HEAD
    zero = jnp.zeros((count, 2 * HEAD), BF16)
    ones = jnp.ones((count, 2 * HEAD), BF16)
    ones_low, ones_high = jnp.where(low, ones, zero), jnp.where(low, zero, ones)

    def part(at):
        return jnp.dot(tokens, proj[:, at : at + WIDE], preferred_element_type=F32).astype(BF16)

    def normed(at, gain):
        values = part(at).astype(F32)
        mean = jnp.dot((values * values).astype(BF16), averager, preferred_element_type=F32)
        return (values * lax.rsqrt(mean + 1e-06) * gain).astype(BF16)

    waits[0]()
    context = []
    for at in range(0, D, WIDE):
        queries = normed(at, gains[query_row : query_row + 1, at : at + WIDE] * (HEAD ** -0.5))
        keys = normed(D + at, gains[query_row + 1 : query_row + 2, at : at + WIDE])
        values = part(2 * D + at)
        for here in range(0, WIDE, 2 * HEAD):
            query = queries[:, here : here + 2 * HEAD]
            key = keys[:, here : here + 2 * HEAD]
            value = values[:, here : here + 2 * HEAD]
            key_pair = jnp.concatenate([jnp.where(low, key, zero), jnp.where(low, zero, key)], axis=0)
            scores = lax.dot_general(query, key_pair, (((1,), (1,)), ((), ())), preferred_element_type=F32)
            raised = jnp.exp(scores).astype(BF16)
            if mask is not None:
                raised = raised * mask
            value_pair = jnp.concatenate(
                [
                    jnp.concatenate([jnp.where(low, value, zero), ones_low], axis=1),
                    jnp.concatenate([jnp.where(low, zero, value), ones_high], axis=1),
                ],
                axis=0,
            )
            both = jnp.dot(raised, value_pair, preferred_element_type=F32)
            context.append((both[:, : 2 * HEAD] / both[:, 2 * HEAD :]).astype(BF16))
    waits[1]()
    return jnp.dot(jnp.concatenate(context, axis=1), out_weight[...], preferred_element_type=F32)


def kernel(
    groups, clips, per, tokens_in_clip,
    frames_ref, norm_ref, space_proj_hbm, space_out_hbm, time_proj_hbm, time_out_hbm, qk_ref,
    block_ref, embed_ref, similar_ref,
    space_proj, space_out, time_proj, time_out,
    outgoing, arrived, branch_out, returned, sums, embeds,
    weight_sem, out_send, out_recv, back_send, back_recv, sum_send, sum_recv, embed_send, embed_recv,
):
    me = lax.axis_index("seq")
    clip = lax.axis_index("clip")
    patches = frames_ref.shape[0]
    padded = outgoing.shape[1]

    loads = [
        pltpu.make_async_copy(source, target, weight_sem.at[at])
        for at, (source, target) in enumerate(
            [(space_proj_hbm, space_proj), (space_out_hbm, space_out), (time_proj_hbm, time_proj), (time_out_hbm, time_out)]
        )
    ]
    for load in loads:
        load.start()

    barrier = pltpu.get_barrier_semaphore()
    each(groups, lambda d: pl.semaphore_signal(
        barrier, inc=1, device_id={"seq": lax.rem(me + d, groups)}, device_id_type=MESH))
    each(clips, lambda d: pl.semaphore_signal(
        barrier, inc=1, device_id={"clip": lax.rem(clip + d, clips)}, device_id_type=MESH))

    def to_group(source, target, send, recv, peer):
        return pltpu.make_async_remote_copy(
            src_ref=source, dst_ref=target, send_sem=send, recv_sem=recv,
            device_id={"seq": peer}, device_id_type=MESH)

    def outward(d):
        peer = lax.rem(me + d, groups)
        return to_group(outgoing.at[peer], arrived.at[d], out_send.at[d], out_recv.at[d], peer)

    def homeward(d):
        peer = lax.rem(me + (groups - d), groups)
        return to_group(branch_out.at[d], returned.at[me], back_send.at[d], back_recv.at[d], peer)

    def share(d):
        return to_group(sums.at[0], sums.at[d], sum_send.at[d], sum_recv.at[d], lax.rem(me + d, groups))

    def announce(d):
        return pltpu.make_async_remote_copy(
            src_ref=embeds.at[clip], dst_ref=embeds.at[clip], send_sem=embed_send.at[d], recv_sem=embed_recv.at[d],
            device_id={"clip": lax.rem(clip + d, clips)}, device_id_type=MESH)

    frames = frames_ref[...].astype(F32)
    spread_out = attend(
        layer_norm(frames, norm_ref[0:1, :]), space_proj, space_out, qk_ref, 0, None,
        (loads[0].wait, loads[1].wait))
    middle = (frames + spread_out).astype(BF16)
    widened = middle.astype(F32)
    ready = layer_norm(widened, norm_ref[1:2, :])
    if padded != per:
        place = lax.broadcasted_iota(jnp.int32, (groups * padded, patches), 0)
        token = lax.broadcasted_iota(jnp.int32, (groups * padded, patches), 1)
        chosen = (token == place // padded * per + place % padded) & (place % padded < per)
        spread = jnp.where(chosen, 1.0, 0.0).astype(BF16)
        ready = jnp.dot(spread, ready, preferred_element_type=F32).astype(BF16)
    outgoing[...] = ready.reshape(outgoing.shape)
    pl.semaphore_wait(barrier, groups - 1 + clips - 1)
    each(groups, lambda d: outward(d).start())
    arrived[0] = outgoing[me]
    own_sum = jnp.sum(widened, axis=0, keepdims=True)

    row = lax.broadcasted_iota(jnp.int32, (groups * per, groups * per), 0) % per
    col = lax.broadcasted_iota(jnp.int32, (groups * per, groups * per), 1) % per
    same = jnp.where(row == col, 1.0, 0.0).astype(BF16)
    each(groups, lambda d: outward(d).wait_recv())
    tokens = arrived[...].reshape(groups * padded, D)
    if padded != per:
        gather = jnp.where(chosen.T, 1.0, 0.0).astype(BF16)
        tokens = jnp.dot(gather, tokens, preferred_element_type=F32).astype(BF16)
    branch = attend(
        tokens, time_proj, time_out, qk_ref, 2, jnp.concatenate([same, same], axis=1),
        (loads[2].wait, loads[3].wait)).astype(BF16)
    sums[0] = own_sum + jnp.sum(branch.astype(F32), axis=0, keepdims=True)
    each(groups, lambda d: share(d).start())
    if padded != per:
        branch = jnp.dot(spread, branch, preferred_element_type=F32).astype(BF16)
    branch_out[...] = branch.reshape(branch_out.shape)
    each(groups, lambda d: homeward(d).start())
    returned[me] = branch_out[0]

    each(groups, lambda d: share(d).wait_recv())
    pooled = jnp.sum(sums[...], axis=0) / tokens_in_clip
    embed = pooled * lax.rsqrt(jnp.mean(pooled * pooled, axis=-1, keepdims=True) + 1e-06)
    embeds[clip] = embed
    each(clips, lambda d: announce(d).start())
    embed_ref[...] = embed

    each(groups, lambda d: homeward(d).wait_recv())
    back = returned[...].reshape(groups * padded, D)
    if padded != per:
        back = jnp.dot(gather, back, preferred_element_type=F32).astype(BF16)
    block_ref[...] = (widened + back.astype(F32)).astype(BF16)

    each(clips, lambda d: announce(d).wait_recv())
    products = jnp.sum(embeds[...] * embed[None], axis=-1, keepdims=True)[:, 0, :] / D
    row = lax.broadcasted_iota(jnp.int32, (clips, clips), 0)
    col = lax.broadcasted_iota(jnp.int32, (clips, clips), 1)
    similar_ref[...] = jnp.sum(jnp.where(row == col, products, 0.0), axis=0, keepdims=True)

    each(groups, lambda d: outward(d).wait_send())
    each(groups, lambda d: share(d).wait_send())
    each(groups, lambda d: homeward(d).wait_send())
    each(clips, lambda d: announce(d).wait_send())


def on_device(frames_in, norm_gains, space_proj, space_out, time_proj, time_out, qk_gains):
    groups, clips = lax.axis_size("seq"), lax.axis_size("clip")
    _, _, patches, channels = frames_in.shape
    per = patches // groups
    padded = -(-per // 16) * 16
    vmem = pl.BlockSpec(memory_space=pltpu.VMEM)
    hbm = pl.BlockSpec(memory_space=pl.ANY)
    blocks = pltpu.VMEM((groups, padded, channels), BF16)
    dma = pltpu.SemaphoreType.DMA
    block, embed, similar = pl.pallas_call(
        functools.partial(kernel, groups, clips, per, patches * groups),
        out_shape=(
            jax.ShapeDtypeStruct((patches, channels), BF16),
            jax.ShapeDtypeStruct((1, channels), F32),
            jax.ShapeDtypeStruct((1, clips), F32),
        ),
        in_specs=[vmem, vmem, hbm, hbm, hbm, hbm, vmem],
        out_specs=(vmem, vmem, vmem),
        scratch_shapes=[
            pltpu.VMEM(space_proj.shape, BF16),
            pltpu.VMEM(space_out.shape, BF16),
            pltpu.VMEM(time_proj.shape, BF16),
            pltpu.VMEM(time_out.shape, BF16),
            blocks, blocks, blocks, blocks,
            pltpu.VMEM((groups, 1, channels), F32),
            pltpu.VMEM((clips, 1, channels), F32),
            dma((4,)),
            dma((groups,)), dma((groups,)), dma((groups,)), dma((groups,)),
            dma((groups,)), dma((groups,)), dma((clips,)), dma((clips,)),
        ],
        compiler_params=pltpu.CompilerParams(
            collective_id=0, has_side_effects=True, vmem_limit_bytes=48 * 1024 * 1024),
    )(frames_in.reshape(patches, channels), norm_gains, space_proj, space_out, time_proj, time_out, qk_gains)
    return block.reshape(frames_in.shape), embed, similar


def solution(mesh):
    return jax.shard_map(
        on_device,
        mesh=mesh,
        in_specs=(P("clip", "seq", None, None), P(), P(), P(), P(), P(), P()),
        out_specs=(P("clip", "seq", None, None), P("clip", None), P("clip", None)),
        check_vma=False,
    )
```

```python
import functools

import jax
import jax.numpy as jnp
from jax import lax
from jax.experimental import pallas as pl
from jax.experimental.pallas import tpu as pltpu
from jax.sharding import PartitionSpec as P

D = 768
HEADS = 12
HEAD = D // HEADS
WIDE = 4 * HEAD
MESH = pl.DeviceIdType.MESH
BF16 = jnp.bfloat16
F32 = jnp.float32


def each(count, body, first=1):
    if count <= 8:
        for at in range(first, count):
            body(at)
    else:
        lax.fori_loop(first, count, lambda at, carry: (body(at), carry)[1], 0)


def layer_norm(widened, gain):
    average = jnp.mean(widened, axis=-1, keepdims=True)
    centred = widened - average
    spread = jnp.mean(centred * centred, axis=-1, keepdims=True)
    return (centred * lax.rsqrt(spread + 1e-05) * gain).astype(BF16)


def attend(tokens, proj, out_weight, gains, query_row, mask, waits):
    row = lax.broadcasted_iota(jnp.int32, (WIDE, WIDE), 0) // HEAD
    col = lax.broadcasted_iota(jnp.int32, (WIDE, WIDE), 1) // HEAD
    averager = jnp.where(row == col, 1.0 / HEAD, 0.0).astype(BF16)
    count = tokens.shape[0]
    low = lax.broadcasted_iota(jnp.int32, (count, 2 * HEAD), 1) < HEAD
    zero = jnp.zeros((count, 2 * HEAD), BF16)
    ones = jnp.ones((count, 2 * HEAD), BF16)
    ones_low, ones_high = jnp.where(low, ones, zero), jnp.where(low, zero, ones)

    def part(at):
        return jnp.dot(tokens, proj[:, at : at + WIDE], preferred_element_type=F32).astype(BF16)

    def normed(at, gain):
        values = part(at).astype(F32)
        mean = jnp.dot((values * values).astype(BF16), averager, preferred_element_type=F32)
        return (values * lax.rsqrt(mean + 1e-06) * gain).astype(BF16)

    context = []
    for at in range(0, D, WIDE):
        waits[at // WIDE]()
        queries = normed(at, gains[query_row : query_row + 1, at : at + WIDE] * (HEAD ** -0.5))
        keys = normed(D + at, gains[query_row + 1 : query_row + 2, at : at + WIDE])
        values = part(2 * D + at)
        for here in range(0, WIDE, 2 * HEAD):
            query = queries[:, here : here + 2 * HEAD]
            key = keys[:, here : here + 2 * HEAD]
            value = values[:, here : here + 2 * HEAD]
            key_pair = jnp.concatenate([jnp.where(low, key, zero), jnp.where(low, zero, key)], axis=0)
            scores = lax.dot_general(query, key_pair, (((1,), (1,)), ((), ())), preferred_element_type=F32)
            raised = jnp.exp(scores).astype(BF16)
            if mask is not None:
                raised = raised * mask
            value_pair = jnp.concatenate(
                [
                    jnp.concatenate([jnp.where(low, value, zero), ones_low], axis=1),
                    jnp.concatenate([jnp.where(low, zero, value), ones_high], axis=1),
                ],
                axis=0,
            )
            both = jnp.dot(raised, value_pair, preferred_element_type=F32)
            context.append((both[:, : 2 * HEAD] / both[:, 2 * HEAD :]).astype(BF16))
    waits[-1]()
    return jnp.dot(jnp.concatenate(context, axis=1), out_weight[...], preferred_element_type=F32)


def kernel(
    groups, clips, per, tokens_in_clip,
    frames_hbm, norm_hbm, space_proj_hbm, space_out_hbm, time_proj_hbm, time_out_hbm, qk_hbm,
    block_ref, embed_ref, similar_ref,
    frames_ref, norm_ref, qk_ref, space_proj, space_out, time_proj, time_out,
    outgoing, arrived, branch_out, returned, sums, embeds,
    load_sem, out_send, out_recv, back_send, back_recv, sum_send, sum_recv, embed_send, embed_recv,
):
    me = lax.axis_index("seq")
    clip = lax.axis_index("clip")
    patches = frames_ref.shape[0]
    padded = outgoing.shape[1]

    pieces = [(frames_hbm, frames_ref), (norm_hbm, norm_ref), (qk_hbm, qk_ref)]
    for source, target, out_source, out_target in (
        (space_proj_hbm, space_proj, space_out_hbm, space_out), (time_proj_hbm, time_proj, time_out_hbm, time_out)):
        for at in range(0, D, WIDE):
            for start in (at, D + at, 2 * D + at):
                columns = pl.ds(start, WIDE)
                pieces.append((source.at[:, columns], target.at[:, columns]))
        pieces.append((out_source, out_target))
    loads = [
        pltpu.make_async_copy(source, target, load_sem.at[at]) for at, (source, target) in enumerate(pieces)]
    for load in loads:
        load.start()

    def waits(first):
        def wait(some):
            for load in some:
                load.wait()
        parts = [loads[first + 3 * at : first + 3 * at + 3] for at in range(D // WIDE)]
        return [functools.partial(wait, part) for part in parts + [loads[first + 9 : first + 10]]]

    barrier = pltpu.get_barrier_semaphore()
    each(groups, lambda d: pl.semaphore_signal(
        barrier, inc=1, device_id={"seq": lax.rem(me + d, groups)}, device_id_type=MESH))
    each(clips, lambda d: pl.semaphore_signal(
        barrier, inc=1, device_id={"clip": lax.rem(clip + d, clips)}, device_id_type=MESH))

    def to_group(source, target, send, recv, peer):
        return pltpu.make_async_remote_copy(
            src_ref=source, dst_ref=target, send_sem=send, recv_sem=recv,
            device_id={"seq": peer}, device_id_type=MESH)

    def outward(d):
        peer = lax.rem(me + d, groups)
        return to_group(outgoing.at[peer], arrived.at[d], out_send.at[d], out_recv.at[d], peer)

    def homeward(d):
        peer = lax.rem(me + (groups - d), groups)
        return to_group(branch_out.at[d], returned.at[me], back_send.at[d], back_recv.at[d], peer)

    def share(d):
        return to_group(sums.at[0], sums.at[d], sum_send.at[d], sum_recv.at[d], lax.rem(me + d, groups))

    def announce(d):
        return pltpu.make_async_remote_copy(
            src_ref=embeds.at[clip], dst_ref=embeds.at[clip], send_sem=embed_send.at[d], recv_sem=embed_recv.at[d],
            device_id={"clip": lax.rem(clip + d, clips)}, device_id_type=MESH)

    for load in loads[:3]:
        load.wait()
    frames = frames_ref[...].astype(F32)
    spread_out = attend(
        layer_norm(frames, norm_ref[0:1, :]), space_proj, space_out, qk_ref, 0, None,
        waits(3))
    middle = (frames + spread_out).astype(BF16)
    widened = middle.astype(F32)
    ready = layer_norm(widened, norm_ref[1:2, :])
    if padded != per:
        place = lax.broadcasted_iota(jnp.int32, (groups * padded, patches), 0)
        token = lax.broadcasted_iota(jnp.int32, (groups * padded, patches), 1)
        chosen = (token == place // padded * per + place % padded) & (place % padded < per)
        spread = jnp.where(chosen, 1.0, 0.0).astype(BF16)
        ready = jnp.dot(spread, ready, preferred_element_type=F32).astype(BF16)
    outgoing[...] = ready.reshape(outgoing.shape)
    pl.semaphore_wait(barrier, groups - 1 + clips - 1)
    each(groups, lambda d: outward(d).start())
    arrived[0] = outgoing[me]
    own_sum = jnp.sum(widened, axis=0, keepdims=True)

    row = lax.broadcasted_iota(jnp.int32, (groups * per, groups * per), 0) % per
    col = lax.broadcasted_iota(jnp.int32, (groups * per, groups * per), 1) % per
    same = jnp.where(row == col, 1.0, 0.0).astype(BF16)
    each(groups, lambda d: outward(d).wait_recv())
    tokens = arrived[...].reshape(groups * padded, D)
    if padded != per:
        gather = jnp.where(chosen.T, 1.0, 0.0).astype(BF16)
        tokens = jnp.dot(gather, tokens, preferred_element_type=F32).astype(BF16)
    branch = attend(
        tokens, time_proj, time_out, qk_ref, 2, jnp.concatenate([same, same], axis=1),
        waits(13)).astype(BF16)
    sums[0] = own_sum + jnp.sum(branch.astype(F32), axis=0, keepdims=True)
    each(groups, lambda d: share(d).start())
    if padded != per:
        branch = jnp.dot(spread, branch, preferred_element_type=F32).astype(BF16)
    branch_out[...] = branch.reshape(branch_out.shape)
    each(groups // 2, lambda d: homeward(d).start())
    returned[me] = branch_out[0]

    each(groups, lambda d: share(d).wait_recv())
    pooled = jnp.sum(sums[...], axis=0) / tokens_in_clip
    embed = pooled * lax.rsqrt(jnp.mean(pooled * pooled, axis=-1, keepdims=True) + 1e-06)
    embeds[clip] = embed
    each(clips, lambda d: announce(d).start())
    each(groups, lambda d: homeward(d).start(), groups // 2)
    embed_ref[...] = embed

    each(groups, lambda d: homeward(d).wait_recv())
    back = returned[...].reshape(groups * padded, D)
    if padded != per:
        back = jnp.dot(gather, back, preferred_element_type=F32).astype(BF16)
    block_ref[...] = (widened + back.astype(F32)).astype(BF16)

    each(clips, lambda d: announce(d).wait_recv())
    products = jnp.sum(embeds[...] * embed[None], axis=-1, keepdims=True)[:, 0, :] / D
    row = lax.broadcasted_iota(jnp.int32, (clips, clips), 0)
    col = lax.broadcasted_iota(jnp.int32, (clips, clips), 1)
    similar_ref[...] = jnp.sum(jnp.where(row == col, products, 0.0), axis=0, keepdims=True)

    each(groups, lambda d: outward(d).wait_send())
    each(groups, lambda d: share(d).wait_send())
    each(groups, lambda d: homeward(d).wait_send())
    each(clips, lambda d: announce(d).wait_send())


def write_out(block_ref, embed_ref, similar_ref, block_hbm, embed_hbm, similar_hbm, store_sem):
    stores = [
        pltpu.make_async_copy(source, target, store_sem.at[at])
        for at, (source, target) in enumerate(
            [(block_ref, block_hbm), (embed_ref, embed_hbm), (similar_ref, similar_hbm)])
    ]
    for store in stores:
        store.start()
    for store in stores:
        store.wait()


def on_device(frames_in, norm_gains, space_proj, space_out, time_proj, time_out, qk_gains):
    groups, clips = lax.axis_size("seq"), lax.axis_size("clip")
    _, _, patches, channels = frames_in.shape
    per = patches // groups
    padded = -(-per // 16) * 16
    vmem = pl.BlockSpec(memory_space=pltpu.VMEM)
    hbm = pl.BlockSpec(memory_space=pltpu.HBM)
    blocks = pltpu.VMEM((groups, padded, channels), BF16)
    dma = pltpu.SemaphoreType.DMA
    block, embed, similar = pl.pallas_call(
        functools.partial(kernel, groups, clips, per, patches * groups),
        out_shape=(
            pltpu.VMEM((patches, channels), BF16), pltpu.VMEM((1, channels), F32), pltpu.VMEM((1, clips), F32)),
        in_specs=[hbm] * 7,
        out_specs=(vmem, vmem, vmem),
        scratch_shapes=[
            pltpu.VMEM((patches, channels), BF16),
            pltpu.VMEM(norm_gains.shape, F32),
            pltpu.VMEM(qk_gains.shape, F32),
            pltpu.VMEM(space_proj.shape, BF16),
            pltpu.VMEM(space_out.shape, BF16),
            pltpu.VMEM(time_proj.shape, BF16),
            pltpu.VMEM(time_out.shape, BF16),
            blocks, blocks, blocks, blocks,
            pltpu.VMEM((groups, 1, channels), F32),
            pltpu.VMEM((clips, 1, channels), F32),
            dma((23,)),
            dma((groups,)), dma((groups,)), dma((groups,)), dma((groups,)),
            dma((groups,)), dma((groups,)), dma((clips,)), dma((clips,)),
        ],
        compiler_params=pltpu.CompilerParams(
            collective_id=0, has_side_effects=True, vmem_limit_bytes=62 * 1024 * 1024),
    )(frames_in.reshape(patches, channels), norm_gains, space_proj, space_out, time_proj, time_out, qk_gains)
    block, embed, similar = pl.pallas_call(
        write_out,
        out_shape=(
            jax.ShapeDtypeStruct((patches, channels), BF16),
            jax.ShapeDtypeStruct((1, channels), F32),
            jax.ShapeDtypeStruct((1, clips), F32),
        ),
        in_specs=[vmem] * 3,
        out_specs=(hbm, hbm, hbm),
        scratch_shapes=[dma((3,))],
        compiler_params=pltpu.CompilerParams(vmem_limit_bytes=1024 * 1024),
    )(block, embed, similar)
    return block.reshape(frames_in.shape), embed, similar


def solution(mesh):
    return jax.shard_map(
        on_device,
        mesh=mesh,
        in_specs=(P("clip", "seq", None, None), P(), P(), P(), P(), P(), P()),
        out_specs=(P("clip", "seq", None, None), P("clip", None), P("clip", None)),
        check_vma=False,
    )
```
